128 devices in a mesh: dp: 32 (over y, z, core), tensor: 4 (over x).
Axes of the slice: x: 4, y: 4, z: 4, core: 2. Of those that a mesh axis runs over, the one named last changes fastest.
Arguments:
- grads: float32 [32, 1024, 8192], P('dp', 'tensor'), may hold values from -6 to 6
- errors: float32 [32, 1024, 8192], P('dp', 'tensor'), may hold values from -6 to 6
- q_start: float32 [8192, 64], replicated, may hold values from -6 to 6
Outputs:
- new_errors: float32 [32, 1024, 8192], P('dp', 'tensor')
- p_orth: float32 [1024, 64], P('tensor')
- q_new: float32 [8192, 64], replicated
The draws below stay inside these ranges and needn't reach their ends.
All inputs are finite; a program needn't handle non-finite values.
Results may differ from the reference program's by a relative error of at most 0.0001.
Values sent between devices are 32-bit elements; how exact they have to be, the bound alone decides.
A program may use at most 128 MiB of HBM per device.

```python
import jax
import jax.numpy as jnp
from jax import lax

COLS = 8192
RANK = 64
ROWS = 1024
REPLICAS = 32
N_DP = 32


def level_of(stream_key, dims, pieces, smallest, largest):
    gain, own = 1.0, jax.random.fold_in(stream_key, 6)
    for position, blocks in pieces:
        heights = jnp.exp(jax.random.uniform(jax.random.fold_in(own, position), (blocks,), jnp.float32, smallest / len(pieces), largest / len(pieces)))
        gain = gain * jnp.repeat(heights, dims[position] // blocks).reshape([-1 if axis == position else 1 for axis in range(len(dims))])
    return gain


def scatter_about(stream_key, shape, width, most, cuts=(), kind=jnp.bfloat16):
    loudness = level_of(stream_key, shape, cuts, -0.22, 0.18) if cuts else 1.0
    values = jax.random.normal(stream_key, shape, jnp.float32) * width * loudness
    return jnp.minimum(jnp.maximum(values, -most), most).astype(kind)


def setup_inputs(seed: int = 0) -> dict:
    key_list = jax.random.split(jax.random.key(seed), 4)
    return {
        "grads": scatter_about(key_list[0], (REPLICAS, ROWS, COLS), 1.0, 6.0, ((0, 32), (1, 4)), jnp.float32),
        "errors": scatter_about(key_list[1], (REPLICAS, ROWS, COLS), 0.5, 6.0, ((0, 32), (1, 4)), jnp.float32),
        "q_start": scatter_about(key_list[2], (COLS, RANK), 1.0, 6.0, (), jnp.float32),
    }


def reference(grads, errors, q_start):
    high = lax.Precision.HIGHEST

    def left_term(carry, pair):
        merged = pair[0] + pair[1]
        return (carry + jnp.dot(merged, q_start, precision=high), None)
    sketch, unused = lax.scan(left_term, jnp.zeros((grads.shape[1], q_start.shape[1]), jnp.float32), (grads, errors))
    sketch = sketch / N_DP
    gram = jnp.dot(sketch.T, sketch, precision=high)
    gram = gram + 1e-05 * (jnp.trace(gram) / gram.shape[0]) * jnp.eye(gram.shape[0], dtype=jnp.float32)
    lower = jnp.linalg.cholesky(gram)
    p_orth = lax.linalg.triangular_solve(lower, sketch, left_side=False, lower=True, transpose_a=True)

    def right_term(carry, pair):
        merged = pair[0] + pair[1]
        return (carry + jnp.dot(merged.T, p_orth, precision=high), None)
    q_new, unused = lax.scan(right_term, jnp.zeros(q_start.shape, jnp.float32), (grads, errors))
    q_new = q_new / N_DP
    approx = jnp.dot(p_orth, q_new.T, precision=high)
    new_errors = grads + errors - approx[None]
    return (new_errors, p_orth, q_new)
```

```python
import functools

import jax
import jax.numpy as jnp
from jax import lax
from jax.experimental import pallas as pl
from jax.experimental.pallas import tpu as pltpu
from jax.sharding import PartitionSpec as P

MESH = pl.DeviceIdType.MESH
F32, BF16 = jnp.float32, jnp.bfloat16
HIGH = lax.Precision.HIGHEST
ROWS, COLS, RANK, HALF = 256, 8192, 64, 32
BLK = 128
NBLK = ROWS // BLK
SLAB = COLS // 4
TILE = 128
GROUPS = ((0, 16), (16, 8), (24, 8))
AXIS_PEERS = [(1, 0, 0), (2, 0, 0), (3, 0, 0), (0, 1, 0), (0, 2, 0), (0, 3, 0), (0, 0, 1), (0, 0, 2), (0, 0, 3)]
ALL_PEERS = [(a, b, c) for a in range(4) for b in range(4) for c in range(4) if (a, b, c) != (0, 0, 0) and 0 in (a, b, c)]


def split(value):
    high = value.astype(BF16)
    return high, (value - high.astype(F32)).astype(BF16)


def device(x, y, z, c):
    return ((y * 4 + z) * 2 + c, x)


def dot_nt(a, b, precision=None):
    return lax.dot_general(a, b, (((1,), (1,)), ((), ())), precision=precision, preferred_element_type=F32)


def exchange(g_hbm, e_hbm, q_hbm, m_ref, z_ref, s_ref, w_ref,
             ebuf, qbuf, qs, hm, spart, sprx, srx, zbuf, zrx, rx1, ph2, rx2, zfin, gsl, lhs,
             in_sem, p_send, p_recv, s_send, s_recv, sp_send, sp_recv, g_send, g_recv,
             zp_send, zp_recv, r1_send, r1_recv, r2_send, r2_recv, a1_send, a1_recv, a2_send, a2_recv,
             f_send, f_recv):
    d = lax.axis_index("dp")
    x = lax.axis_index("tensor")
    y, z, c = d // 8, (d // 2) % 4, d % 2
    me = y * 4 + z
    partner = device(x, y, z, 1 - c)
    mine = pl.multiple_of(c * HALF, HALF)
    other = pl.multiple_of((1 - c) * HALF, HALF)

    def remote(src, dst, send, recv, target):
        return pltpu.make_async_remote_copy(src_ref=src, dst_ref=dst, send_sem=send, recv_sem=recv, device_id=target, device_id_type=MESH)

    loads = {}
    for b in range(NBLK):
        for k in range(4):
            rows, cols = pl.ds(b * BLK, BLK), pl.ds(k * SLAB, SLAB)
            parts = []
            if b == 0:
                parts.append(pltpu.make_async_copy(q_hbm.at[:, cols], qbuf.at[:, cols], in_sem.at[k, 2]))
            parts.append(pltpu.make_async_copy(g_hbm.at[rows, cols], m_ref.at[rows, cols], in_sem.at[b * 4 + k, 0]))
            parts.append(pltpu.make_async_copy(e_hbm.at[rows, cols], ebuf.at[rows, cols], in_sem.at[b * 4 + k, 1]))
            for part in parts:
                part.start()
            loads[b, k] = parts

    barrier = pltpu.get_barrier_semaphore()
    pl.semaphore_signal(barrier, inc=1, device_id=partner, device_id_type=MESH)
    for dx, dy, dz in ALL_PEERS:
        pl.semaphore_signal(barrier, inc=1, device_id=device((x + dx) % 4, (y + dy) % 4, (z + dz) % 4, c), device_id_type=MESH)

    def left_block(b, k):
        for part in loads[b, k]:
            part.wait()

        @pl.loop(0, SLAB // 256)
        def _(i):
            cols = pl.ds(pl.multiple_of(k * SLAB + i * 256, 256), 256)
            if b == 0:
                q_high, q_mid = split(qbuf[:, cols])
                qs[0:RANK, cols] = q_high
                qs[RANK:, cols] = q_mid
            rows = slice(b * BLK, (b + 1) * BLK)
            merged = m_ref[rows, cols] + ebuf[rows, cols]
            m_ref[rows, cols] = merged
            high, mid = split(merged)
            hm[b, 0:BLK, cols] = high
            hm[b, BLK:, cols] = mid

        cols = slice(k * SLAB, (k + 1) * SLAB)
        return dot_nt(qs[:, cols], hm[b, :, cols])

    def pair_copy(b):
        return remote(spart.at[b, pl.ds(other, HALF)], sprx.at[b], p_send.at[b], p_recv.at[b], partner)

    def left_send(b):
        copy = pair_copy(b)
        copy.wait()
        srx[b, me] = spart[b, pl.ds(mine, HALF)] + sprx[b]

        @pl.loop(1, 16)
        def _(r):
            target = device(x, (y + r // 4) % 4, (z + r % 4) % 4, c)
            remote(srx.at[b, me], srx.at[b, me], s_send.at[b], s_recv.at[b], target).start()

    for b in range(NBLK):
        total = jnp.zeros((2 * RANK, 2 * BLK), F32)
        for k in range(4):
            total = total + left_block(b, k)
            if b > 0 and k == 0:
                left_send(b - 1)
        total = total[:RANK] + total[RANK:]
        spart[b] = total[:, :BLK] + total[:, BLK:]
        if b == 0:
            pl.semaphore_wait(barrier, 1 + len(ALL_PEERS))
        pair_copy(b).start()
    left_send(NBLK - 1)

    def whole_copy(b):
        place = (pl.ds(mine, HALF), pl.ds(b * BLK, BLK))
        return remote(s_ref.at[place], s_ref.at[place], sp_send.at[b], sp_recv.at[b], partner)

    for b in range(NBLK):
        fifteen = srx.at[b, pl.ds(0, 15)]
        pltpu.make_async_copy(fifteen, fifteen, s_recv.at[b]).wait()
        pltpu.make_async_copy(fifteen, fifteen, s_send.at[b]).wait()
        total = srx[b, 0]
        for r in range(1, 16):
            total = total + srx[b, r]
        s_ref[pl.ds(mine, HALF), b * BLK:(b + 1) * BLK] = total * (1.0 / 32)
        whole_copy(b).start()
    for b in range(NBLK):
        whole_copy(b).wait()

    sketch = s_ref[...]
    high, mid = split(sketch)
    both = jnp.concatenate([high, mid], axis=0)
    for b in range(NBLK):
        part = both[:, b * BLK:(b + 1) * BLK]
        lhs[b] = jnp.concatenate([part, part], axis=1)

    gsl[x] = jnp.concatenate([dot_nt(sketch, sketch, HIGH), jnp.zeros((RANK, RANK), F32)], axis=1)
    for k in range(3):
        remote(gsl.at[x], gsl.at[x], g_send, g_recv, device((x + k + 1) % 4, y, z, c)).start()

    first = (jnp.where(c == 0, x, y), jnp.where(c == 0, y, x), z)

    def moved(g, da, db, dc):
        if g == 2:
            return device((x + db) % 4, (y + dc) % 4, (z + da) % 4, c)
        flip = c if g == 0 else 1 - c
        dx = jnp.where(flip == 0, da, dc)
        dy = jnp.where(flip == 0, db, da)
        dz = jnp.where(flip == 0, dc, db)
        return device((x + dx) % 4, (y + dy) % 4, (z + dz) % 4, c)

    xy0, xy1 = c == 0, c == 1
    second = (jnp.where(c == 0, y, z), jnp.where(c == 0, z, y), x)
    third = (jnp.where(c == 0, z, x), jnp.where(c == 0, x, z), y)

    def zpair(s, k):
        cols = pl.ds(pl.multiple_of(k * SLAB, SLAB), SLAB)
        return remote(zbuf.at[pl.ds(other, HALF), cols], zrx.at[s], zp_send.at[s], zp_recv.at[s], partner)

    def order(s):
        return lax.rem(x + y + z + s, 4)

    def slab_sum(s):
        k = order(s)
        zpair(s, k).wait()

        @pl.loop(0, SLAB // 512)
        def _(i):
            here = pl.ds(pl.multiple_of(i * 512, 512), 512)
            cols = pl.ds(pl.multiple_of(k * SLAB + i * 512, 512), 512)
            zbuf[pl.ds(mine, HALF), cols] += zrx[s, :, here]

        for g, (row, rows) in enumerate(GROUPS):
            step = lax.rem(k - first[g] + 4, 4)

            @pl.when(step != 0)
            def _():
                src = zbuf.at[pl.ds(pl.multiple_of(mine + row, 8), rows), pl.ds(pl.multiple_of(k * SLAB, SLAB), SLAB)]
                dst = rx1.at[step - 1, pl.ds(row, rows)]
                remote(src, dst, r1_send.at[g], r1_recv.at[g], moved(g, step, 0, 0)).start()

    for s in range(4):
        k = order(s)

        @pl.loop(0, SLAB // 256)
        def _(i):
            cols = pl.ds(pl.multiple_of(k * SLAB + i * 256, 256), 256)
            total = jnp.dot(lhs[0], hm[0, :, cols], preferred_element_type=F32)
            for b in range(1, NBLK):
                total = total + jnp.dot(lhs[b], hm[b, :, cols], preferred_element_type=F32)
            zbuf[:, cols] = total[:RANK] + total[RANK:]

        zpair(s, k).start()
        if s > 0:
            slab_sum(s - 1)
    slab_sum(3)

    for g, (row, rows) in enumerate(GROUPS):
        three = rx1.at[pl.ds(0, 3), pl.ds(row, rows)]
        pltpu.make_async_copy(three, three, r1_recv.at[g]).wait()
        cols = pl.ds(pl.multiple_of(first[g] * SLAB, SLAB), SLAB)
        ph2[row:row + rows] = (
            (zbuf[pl.ds(pl.multiple_of(mine + row, 8), rows), cols] + rx1[0, row:row + rows])
            + (rx1[1, row:row + rows] + rx1[2, row:row + rows])
        )

        @pl.loop(1, 16)
        def _(r):
            db, dc = r // 4, r % 4
            tile = lax.rem(second[g] + db, 4) * 4 + lax.rem(third[g] + dc, 4)
            src = ph2.at[pl.ds(row, rows), pl.ds(pl.multiple_of(tile * TILE, TILE), TILE)]
            remote(src, rx2.at[r - 1, pl.ds(row, rows)], r2_send.at[g], r2_recv.at[g], moved(g, 0, db, dc)).start()

    three = gsl.at[pl.ds(0, 3)]
    pltpu.make_async_copy(three, three, g_recv).wait()
    pltpu.make_async_copy(three, three, g_send).wait()
    gram = (gsl[0] + gsl[1]) + (gsl[2] + gsl[3])
    lane = lax.broadcasted_iota(jnp.int32, (RANK, 2 * RANK), 1)
    sub = lax.broadcasted_iota(jnp.int32, (RANK, 2 * RANK), 0)
    diagonal = jnp.where(lane == sub, gram, 0.0)
    trace = jnp.sum(jnp.sum(diagonal, axis=1, keepdims=True), axis=0, keepdims=True)
    mat = gram + jnp.where(lane == sub, 1e-05 * (trace / RANK), 0.0) + jnp.where(lane == sub + RANK, 1.0, 0.0)
    row_id = lax.broadcasted_iota(jnp.int32, (RANK, 1), 0)
    for j in range(RANK):
        pivot = mat[j:j + 1, :]
        factor = jnp.where(row_id > j, mat[:, j:j + 1] / mat[j:j + 1, j:j + 1], 0.0)
        mat = mat - factor * pivot
    scale = jnp.sum(jnp.where(lane == sub, mat, 0.0), axis=1, keepdims=True)
    w_ref[...] = mat[:, RANK:] / jnp.sqrt(scale)

    for g, (row, rows) in enumerate(GROUPS):
        fifteen = rx2.at[pl.ds(0, 15), pl.ds(row, rows)]
        pltpu.make_async_copy(fifteen, fifteen, r2_recv.at[g]).wait()
        tile = second[g] * 4 + third[g]
        total = ph2[row:row + rows, pl.ds(pl.multiple_of(tile * TILE, TILE), TILE)]
        for r in range(15):
            total = total + rx2[r, row:row + rows]
        place = (pl.ds(pl.multiple_of(mine + row, 8), rows), pl.ds(pl.multiple_of(first[g] * SLAB + tile * TILE, TILE), TILE))
        z_ref[place] = total

        @pl.loop(1, 16)
        def _(r):
            remote(z_ref.at[place], z_ref.at[place], a1_send.at[g], a1_recv.at[g], moved(g, 0, r // 4, r % 4)).start()

    def slab(g, v):
        row, rows = GROUPS[g]
        return z_ref.at[pl.ds(pl.multiple_of(mine + row, 8), rows), pl.ds(pl.multiple_of(v * SLAB, SLAB), SLAB)]

    def forward(g, step):
        here = slab(g, lax.rem(first[g] + step, 4))
        return remote(here, here, f_send.at[g, step], f_recv.at[g, step], partner)

    def along(g, step):
        here = slab(g, first[g])
        return remote(here, here, a2_send.at[g, step - 1], a2_recv.at[g, step - 1], moved(g, step, 0, 0))

    for g, (row, rows) in enumerate(GROUPS):
        fifteen = z_ref.at[pl.ds(pl.multiple_of(mine + row, 8), rows), pl.ds(0, 15 * TILE)]
        pltpu.make_async_copy(fifteen, fifteen, a1_recv.at[g]).wait()
        for step in (2, 1, 3):
            along(g, step).start()
        forward(g, 0).start()
    for step in (1, 3, 2):
        for g in range(3):
            along(g, step).wait_recv()
            forward(g, 4 - step).start()

    for g, (row, rows) in enumerate(GROUPS):
        three = rx1.at[pl.ds(0, 3), pl.ds(row, rows)]
        pltpu.make_async_copy(three, three, r1_send.at[g]).wait()
        fifteen = rx2.at[pl.ds(0, 15), pl.ds(row, rows)]
        pltpu.make_async_copy(fifteen, fifteen, r2_send.at[g]).wait()
        fifteen = z_ref.at[pl.ds(pl.multiple_of(mine + row, 8), rows), pl.ds(0, 15 * TILE)]
        pltpu.make_async_copy(fifteen, fifteen, a1_send.at[g]).wait()
        for step in (1, 2, 3):
            along(g, step).wait_send()
    for step in range(4):
        for g in range(3):
            forward(g, step).wait()


def finish(m_ref, z_ref, s_ref, w_ref, n_hbm, p_hbm, q_hbm, nbuf, pbuf, qbuf, sem):
    chunk = 1024
    w = w_ref[...]
    p_t = jnp.dot(w, s_ref[...], precision=HIGH, preferred_element_type=F32)
    pbuf[...] = p_t
    copies = [pltpu.make_async_copy(pbuf, p_hbm, sem.at[0, 2])]
    copies[0].start()
    w_high, w_mid = split(w * (1.0 / 32))
    w_cat = jnp.concatenate([w_high, w_high, w_mid, w_mid], axis=1)
    p_high, p_mid = split(p_t.T)
    p_cat = jnp.concatenate([p_high, p_high, p_mid, p_mid], axis=1)
    for k in range(COLS // chunk):
        @pl.loop(0, chunk // 256)
        def _(i):
            cols = pl.ds(pl.multiple_of(k * chunk + i * 256, 256), 256)
            z_high, z_mid = split(z_ref[:, cols])
            q = jnp.dot(w_cat, jnp.concatenate([z_high, z_mid, z_high, z_mid], axis=0), preferred_element_type=F32)
            qbuf[:, cols] = q
            q_high, q_mid = split(q)
            approx = jnp.dot(p_cat, jnp.concatenate([q_high, q_mid, q_high, q_mid], axis=0), preferred_element_type=F32)
            nbuf[:, cols] = m_ref[:, cols] - approx

        cols = pl.ds(k * chunk, chunk)
        copies.append(pltpu.make_async_copy(nbuf.at[:, cols], n_hbm.at[:, cols], sem.at[k, 0]))
        copies.append(pltpu.make_async_copy(qbuf.at[:, cols], q_hbm.at[:, cols], sem.at[k, 1]))
        copies[-2].start()
        copies[-1].start()
    for copy in copies:
        copy.wait()


def local(grads, errors, q_start):
    vmem = pl.BlockSpec(memory_space=pltpu.VMEM)
    hbm = pl.BlockSpec(memory_space=pl.ANY)
    dma = pltpu.SemaphoreType.DMA
    merged, z_sum, sketch, w = pl.pallas_call(
        exchange,
        out_shape=(pltpu.VMEM((ROWS, COLS), F32), pltpu.VMEM((RANK, COLS), F32), pltpu.VMEM((RANK, ROWS), F32), pltpu.VMEM((RANK, RANK), F32)),
        in_specs=[hbm] * 3,
        out_specs=(vmem,) * 4,
        scratch_shapes=[
            pltpu.VMEM((ROWS, COLS), F32),
            pltpu.VMEM((RANK, COLS), F32),
            pltpu.VMEM((2 * RANK, COLS), BF16),
            pltpu.VMEM((NBLK, 2 * BLK, COLS), BF16),
            pltpu.VMEM((NBLK, RANK, BLK), F32),
            pltpu.VMEM((NBLK, HALF, BLK), F32),
            pltpu.VMEM((NBLK, 16, HALF, BLK), F32),
            pltpu.VMEM((RANK, COLS), F32),
            pltpu.VMEM((4, HALF, SLAB), F32),
            pltpu.VMEM((3, HALF, SLAB), F32),
            pltpu.VMEM((HALF, SLAB), F32),
            pltpu.VMEM((15, HALF, TILE), F32),
            pltpu.VMEM((HALF, TILE), F32),
            pltpu.VMEM((4, RANK, 2 * RANK), F32),
            pltpu.VMEM((NBLK, 2 * RANK, 2 * BLK), BF16),
            dma((4 * NBLK, 3)),
            dma((NBLK,)), dma((NBLK,)), dma((NBLK,)), dma((NBLK,)), dma((NBLK,)), dma((NBLK,)), dma(()), dma(()),
            dma((4,)), dma((4,)), dma((3,)), dma((3,)), dma((3,)), dma((3,)), dma((3,)), dma((3,)), dma((3, 3)), dma((3, 3)),
            dma((3, 4)), dma((3, 4)),
        ],
        compiler_params=pltpu.CompilerParams(collective_id=0, has_side_effects=True, vmem_limit_bytes=36 << 20),
        name="exchange",
    )(grads[0], errors[0], q_start.T)
    new_errors, p_t, q_t = pl.pallas_call(
        finish,
        out_shape=(jax.ShapeDtypeStruct((ROWS, COLS), F32), jax.ShapeDtypeStruct((RANK, ROWS), F32), jax.ShapeDtypeStruct((RANK, COLS), F32)),
        in_specs=[vmem] * 4,
        out_specs=(hbm,) * 3,
        scratch_shapes=[pltpu.VMEM((ROWS, COLS), F32), pltpu.VMEM((RANK, ROWS), F32), pltpu.VMEM((RANK, COLS), F32), dma((8, 3))],
        compiler_params=pltpu.CompilerParams(vmem_limit_bytes=24 << 20),
        name="finish",
    )(merged, z_sum, sketch, w)
    return new_errors[None], p_t.T, q_t.T


def solution(mesh):
    return jax.shard_map(
        local,
        mesh=mesh,
        in_specs=(P("dp", "tensor", None), P("dp", "tensor", None), P()),
        out_specs=(P("dp", "tensor", None), P("tensor", None), P()),
        check_vma=False,
    )
```

```python
import jax
import jax.numpy as jnp
from jax import lax
from jax.experimental import pallas as pl
from jax.experimental.pallas import tpu as pltpu
from jax.sharding import PartitionSpec as P

MESH = pl.DeviceIdType.MESH
F32, BF16 = jnp.float32, jnp.bfloat16
HIGH = lax.Precision.HIGHEST
ROWS, COLS, RANK, HALF = 256, 8192, 64, 32
BLK = 128
NBLK = ROWS // BLK
CHUNKS = ((1024,) * 8, (1024,) * 7 + (512, 256, 256))
OWN = COLS // 2
SLAB = OWN // 4
STRIP = SLAB // 4
TILE = 128
GROUPS = range(4)
GROUP = 16
PIECES = (512,) * 16
AROUND = [(a, b, c) for a in range(4) for b in range(4) for c in range(4) if (a, b, c) != (0, 0, 0) and 0 in (a, b, c)]


def split(value):
    high = value.astype(BF16)
    return high, (value - high.astype(F32)).astype(BF16)


def mod4(value):
    return lax.rem(value, 4)


def device(x, y, z, c):
    return ((y * 4 + z) * 2 + c, x)


def dot_nt(a, b, precision=None):
    return lax.dot_general(a, b, (((1,), (1,)), ((), ())), precision=precision, preferred_element_type=F32)


def exchange(g_hbm, e_hbm, q_hbm, m_ref, z_ref, p_ref, pcat_ref, wcat_ref,
             ebuf, qbuf, qs, hm, mrx, hm2, spart, sprx, srx, s_ref, lhs, zbuf, rx1, ph2, rx2, gsl,
             in_sem, m_send, m_recv, p_send, p_recv, s_send, s_recv, sp_send, sp_recv, g_send, g_recv,
             r1_send, r1_recv, r2_send, r2_recv, a1_send, a1_recv, a2_send, a2_recv, f_send, f_recv):
    d = lax.axis_index("dp")
    x = lax.axis_index("tensor")
    y, z, c = lax.div(d, 8), mod4(lax.div(d, 2)), lax.rem(d, 2)
    me = y * 4 + z
    partner = device(x, y, z, 1 - c)
    mine = pl.multiple_of(c * HALF, HALF)
    other = pl.multiple_of((1 - c) * HALF, HALF)
    own = pl.multiple_of(c * OWN, OWN)
    theirs = pl.multiple_of((1 - c) * OWN, OWN)

    def remote(src, dst, send, recv, target):
        return pltpu.make_async_remote_copy(src_ref=src, dst_ref=dst, send_sem=send, recv_sem=recv, device_id=target, device_id_type=MESH)

    def all_of(ref, sem):
        pltpu.make_async_copy(ref, ref, sem).wait()

    loads = {}
    for b in range(NBLK):
        begin = 0
        for k, size in enumerate(CHUNKS[b]):
            rows, cols = pl.ds(b * BLK, BLK), pl.ds(begin, size)
            sems = in_sem.at[b * len(CHUNKS[0]) + k]
            parts = [
                pltpu.make_async_copy(g_hbm.at[rows, cols], m_ref.at[rows, cols], sems.at[0]),
                pltpu.make_async_copy(e_hbm.at[rows, cols], ebuf.at[rows, cols], sems.at[1]),
            ]
            if b == 0:
                parts.append(pltpu.make_async_copy(q_hbm.at[:, cols], qbuf.at[:, cols], sems.at[2]))
            for part in parts:
                part.start()
            loads[b, k] = begin, size, parts
            begin += size

    barrier = pltpu.get_barrier_semaphore()
    pl.semaphore_signal(barrier, inc=1, device_id=partner, device_id_type=MESH)
    for dx, dy, dz in AROUND:
        pl.semaphore_signal(barrier, inc=1, device_id=device(mod4(x + dx), mod4(y + dy), mod4(z + dz), c), device_id_type=MESH)

    def left_chunk(b, k):
        begin, size, parts = loads[b, k]
        for part in parts:
            part.wait()
        rows = slice(b * BLK, (b + 1) * BLK)
        for i in range(0, size, 256):
            cols = slice(begin + i, begin + i + 256)
            if b == 0:
                qs[0:RANK, cols], qs[RANK:, cols] = split(qbuf[:, cols])
            merged = m_ref[rows, cols] + ebuf[rows, cols]
            m_ref[rows, cols] = merged
            hm[k % 2, 0:BLK, i:i + 256], hm[k % 2, BLK:, i:i + 256] = split(merged)
        return dot_nt(qs[:, begin:begin + size], hm[k % 2, :, :size])

    def pair_copy(b):
        return remote(spart.at[b, pl.ds(other, HALF)], sprx.at[b], p_send.at[b], p_recv.at[b], partner)

    def merged_copy(b):
        rows = pl.ds(b * BLK, BLK)
        return remote(m_ref.at[rows, pl.ds(theirs, OWN)], mrx.at[rows], m_send.at[b], m_recv.at[b], partner)

    def left_send(b):
        pair_copy(b).wait()
        srx[b, me] = spart[b, pl.ds(mine, HALF)] + sprx[b]

        @pl.loop(1, 16)
        def _(r):
            target = device(x, mod4(y + lax.div(r, 4)), mod4(z + mod4(r)), c)
            remote(srx.at[b, me], srx.at[b, me], s_send.at[b], s_recv.at[b], target).start()

    for b in range(NBLK):
        total = jnp.zeros((2 * RANK, 2 * BLK), F32)
        for k in range(len(CHUNKS[b])):
            total = total + left_chunk(b, k)
            if b > 0 and k == 1:
                left_send(b - 1)
        total = total[:RANK] + total[RANK:]
        spart[b] = total[:, :BLK] + total[:, BLK:]
        if b == 0:
            pl.semaphore_wait(barrier, 1 + len(AROUND))
        pair_copy(b).start()
        merged_copy(b).start()
    left_send(NBLK - 1)

    def left_sum(b):
        fifteen = srx.at[b, pl.ds(0, 15)]
        all_of(fifteen, s_recv.at[b])
        total = srx[b, 0]
        for r in range(1, 16):
            total = total + srx[b, r]
        place = (pl.ds(mine, HALF), pl.ds(b * BLK, BLK))
        s_ref[pl.ds(mine, HALF), b * BLK:(b + 1) * BLK] = total * (1.0 / 32)
        copy = remote(s_ref.at[place], s_ref.at[place], sp_send.at[b], sp_recv.at[b], partner)
        copy.start()
        return copy

    def chip_sum(b):
        merged_copy(b).wait()

        @pl.loop(0, OWN // 256, unroll=4)
        def _(i):
            here = pl.ds(pl.multiple_of(i * 256, 256), 256)
            there = pl.ds(pl.multiple_of(own + i * 256, 256), 256)
            rows = slice(b * BLK, (b + 1) * BLK)
            hm2[b, 0:BLK, here], hm2[b, BLK:, here] = split(m_ref[rows, there] + mrx[rows, here])

    def left_ready(b, copy):
        copy.wait()
        high, mid = split(s_ref[:, b * BLK:(b + 1) * BLK])
        both = jnp.concatenate([high, mid], axis=0)
        lhs[b] = jnp.concatenate([both, both], axis=1)

    def right_part(b, cols):
        total = jnp.dot(lhs[b], hm2[b, :, cols], preferred_element_type=F32)
        return total[:RANK] + total[RANK:]

    copy = left_sum(0)
    chip_sum(0)
    left_ready(0, copy)
    for i in range(0, OWN, 512):
        zbuf[:, i:i + 512] = right_part(0, slice(i, i + 512))
    chip_sum(1)
    copy = left_sum(1)
    left_ready(1, copy)

    def by_turn(g, options):
        if g < 3:
            return options[g]
        return jnp.where(c == 0, options[0], options[1])

    first = [by_turn(g, (x, y, z)) for g in GROUPS]
    second = [by_turn(g, (y, z, x)) for g in GROUPS]
    third = [by_turn(g, (z, x, y)) for g in GROUPS]

    def moved(g, da, db, dc):
        dx, dy, dz = by_turn(g, (da, dc, db)), by_turn(g, (db, da, dc)), by_turn(g, (dc, db, da))
        return device(mod4(x + dx), mod4(y + dy), mod4(z + dz), c)

    def group_rows(g):
        return pl.ds(g * GROUP, GROUP)

    for i in range(0, OWN, 512):
        zbuf[:, i:i + 512] += right_part(1, slice(i, i + 512))

    for step in (2, 1, 3):
        for g in GROUPS:
            k = mod4(first[g] + step)
            src = zbuf.at[group_rows(g), pl.ds(pl.multiple_of(k * SLAB, SLAB), SLAB)]
            remote(src, rx1.at[step - 1, group_rows(g)], r1_send.at[g], r1_recv.at[g], moved(g, step, 0, 0)).start()

    sketch = s_ref[...]
    gsl[x] = jnp.concatenate([dot_nt(sketch, sketch, HIGH), jnp.zeros((RANK, RANK), F32)], axis=1)
    for k in range(3):
        remote(gsl.at[x], gsl.at[x], g_send, g_recv, device(mod4(x + k + 1), y, z, c)).start()

    def tile_of(v, w):
        return pl.ds(pl.multiple_of(lax.rem(w, 2) * 8, 8), 8), pl.multiple_of((v * 2 + lax.div(w, 2)) * TILE, TILE)

    for g in GROUPS:
        all_of(rx1.at[pl.ds(0, 3), group_rows(g)], r1_recv.at[g])
        cols = pl.ds(pl.multiple_of(first[g] * SLAB, SLAB), SLAB)
        rows = slice(g * GROUP, (g + 1) * GROUP)
        ph2[g] = (zbuf[rows, cols] + rx1[0, rows]) + (rx1[1, rows] + rx1[2, rows])

        @pl.loop(1, 16)
        def _(r):
            db, dc = lax.div(r, 4), mod4(r)
            rows, col = tile_of(mod4(second[g] + db), mod4(third[g] + dc))
            remote(ph2.at[g, rows, pl.ds(col, TILE)], rx2.at[g, r - 1], r2_send.at[g], r2_recv.at[g], moved(g, 0, db, dc)).start()

    three = gsl.at[pl.ds(0, 3)]
    all_of(three, g_recv)
    gram = (gsl[0] + gsl[1]) + (gsl[2] + gsl[3])
    lane = lax.broadcasted_iota(jnp.int32, (RANK, 2 * RANK), 1)
    sub = lax.broadcasted_iota(jnp.int32, (RANK, 2 * RANK), 0)
    diagonal = jnp.where(lane == sub, gram, 0.0)
    trace = jnp.sum(jnp.sum(diagonal, axis=1, keepdims=True), axis=0, keepdims=True)
    mat = gram + jnp.where(lane == sub, 1e-05 * (trace / RANK), 0.0) + jnp.where(lane == sub + RANK, 1.0, 0.0)
    row_id = lax.broadcasted_iota(jnp.int32, (RANK, 1), 0)

    def eliminate(mat, begin, end):
        for j in range(begin, end):
            pivot = mat[j:j + 1, :]
            factor = jnp.where(row_id > j, mat[:, j:j + 1] / mat[j:j + 1, j:j + 1], 0.0)
            mat = mat - factor * pivot
        return mat

    mat = eliminate(mat, 0, RANK // 2)

    for g in GROUPS:
        all_of(rx2.at[g], r2_recv.at[g])
        rows, col = tile_of(second[g], third[g])
        total = ph2[g, rows, pl.ds(col, TILE)]
        for r in range(15):
            total = total + rx2[g, r]
        rows = pl.ds(pl.multiple_of(g * GROUP + lax.rem(third[g], 2) * 8, 8), 8)
        place = (rows, pl.ds(pl.multiple_of(own + first[g] * SLAB + col, TILE), TILE))
        z_ref[place] = total

        @pl.loop(1, 16)
        def _(r):
            remote(z_ref.at[place], z_ref.at[place], a1_send.at[g], a1_recv.at[g, lax.div(r, 4)], moved(g, 0, lax.div(r, 4), mod4(r))).start()

    mat = eliminate(mat, RANK // 2, RANK)
    scale = jnp.sum(jnp.where(lane == sub, mat, 0.0), axis=1, keepdims=True)
    inverse = mat[:, RANK:] / jnp.sqrt(scale)
    parts = jnp.concatenate(split(inverse * (1.0 / 32)), axis=0)
    wcat_ref[...] = jnp.concatenate([parts, parts], axis=1)

    def slab(g, v):
        return z_ref.at[group_rows(g), pl.ds(pl.multiple_of(own + v * SLAB, SLAB), SLAB)]

    def forward(g, step):
        here = slab(g, mod4(first[g] + step))
        return remote(here, here, f_send.at[g, step], f_recv.at[g, step], partner)

    def along(g, step, away):
        cols = pl.ds(pl.multiple_of(own + first[g] * SLAB + mod4(second[g] + 4 - away) * STRIP, STRIP), STRIP)
        here = z_ref.at[group_rows(g), cols]
        return remote(here, here, a2_send.at[g, step - 1], a2_recv.at[g, step - 1], moved(g, step, 0, 0))

    fifteen = [z_ref.at[pl.ds(g * GROUP, 8), pl.ds(0, 15 * TILE)] for g in GROUPS]
    for away in (0, 1, 3, 2):
        for g in GROUPS:
            all_of(z_ref.at[pl.ds(g * GROUP, 8), pl.ds(0, (4 if away else 3) * TILE)], a1_recv.at[g, away])
            for step in (2, 1, 3):
                along(g, step, away).start()
    for g in GROUPS:
        forward(g, 0).start()
    p_t = jnp.dot(inverse, sketch, precision=HIGH, preferred_element_type=F32)
    p_ref[...] = p_t
    high, mid = split(p_t.T)
    pcat_ref[...] = jnp.concatenate([high, high, mid], axis=1)
    for step in (1, 3, 2):
        for g in GROUPS:
            all_of(slab(g, 0), a2_recv.at[g, step - 1])
            forward(g, 4 - step).start()

    for b in range(NBLK):
        all_of(srx.at[b, pl.ds(0, 15)], s_send.at[b])
    all_of(three, g_send)
    for g in GROUPS:
        all_of(rx1.at[pl.ds(0, 3), group_rows(g)], r1_send.at[g])
        all_of(rx2.at[g], r2_send.at[g])
        all_of(fifteen[g], a1_send.at[g])
        for step in (1, 2, 3):
            all_of(slab(g, 0), a2_send.at[g, step - 1])
    for step in range(4):
        for g in GROUPS:
            forward(g, step).wait()


def finish(m_ref, z_ref, p_ref, pcat_ref, wcat_ref, n_hbm, p_hbm, q_hbm, nbuf, qbuf, sem):
    copies = []

    def write(k, cols, q3):
        nbuf[:, cols] = m_ref[:, cols] - jnp.dot(pcat_ref[...], q3, preferred_element_type=F32)
        copies.append(pltpu.make_async_copy(nbuf.at[:, cols], n_hbm.at[:, cols], sem.at[k, 0]))
        copies[-1].start()

    begin, last = 0, None
    for k, size in enumerate(PIECES):
        cols = pl.ds(begin, size)
        begin += size
        q = jnp.dot(wcat_ref[...], jnp.concatenate(split(z_ref[:, cols]), axis=0), preferred_element_type=F32)
        q = q[:RANK] + q[RANK:]
        qbuf[:, cols] = q
        high, mid = split(q)
        q3 = jnp.concatenate([high, mid, high], axis=0)
        if last is not None:
            write(*last)
        last = (k, cols, q3)
    copies.append(pltpu.make_async_copy(qbuf, q_hbm, sem.at[0, 1]))
    copies[-1].start()
    write(*last)
    copies.append(pltpu.make_async_copy(p_ref, p_hbm, sem.at[0, 2]))
    copies[-1].start()
    for copy in copies:
        copy.wait()


def local(grads, errors, q_start):
    vmem = pl.BlockSpec(memory_space=pltpu.VMEM)
    hbm = pl.BlockSpec(memory_space=pl.ANY)
    dma = pltpu.SemaphoreType.DMA
    parts = pl.pallas_call(
        exchange,
        out_shape=(
            pltpu.VMEM((ROWS, COLS), F32), pltpu.VMEM((RANK, COLS), F32), pltpu.VMEM((RANK, ROWS), F32),
            pltpu.VMEM((ROWS, 3 * RANK), BF16), pltpu.VMEM((2 * RANK, 2 * RANK), BF16),
        ),
        in_specs=[hbm] * 3,
        out_specs=(vmem,) * 5,
        scratch_shapes=[
            pltpu.VMEM((ROWS, COLS), F32),
            pltpu.VMEM((RANK, COLS), F32),
            pltpu.VMEM((2 * RANK, COLS), BF16),
            pltpu.VMEM((2, 2 * BLK, max(CHUNKS[0])), BF16),
            pltpu.VMEM((ROWS, OWN), F32),
            pltpu.VMEM((NBLK, 2 * BLK, OWN), BF16),
            pltpu.VMEM((NBLK, RANK, BLK), F32),
            pltpu.VMEM((NBLK, HALF, BLK), F32),
            pltpu.VMEM((NBLK, 16, HALF, BLK), F32),
            pltpu.VMEM((RANK, ROWS), F32),
            pltpu.VMEM((NBLK, 2 * RANK, 2 * BLK), BF16),
            pltpu.VMEM((RANK, OWN), F32),
            pltpu.VMEM((3, RANK, SLAB), F32),
            pltpu.VMEM((4, GROUP, SLAB), F32),
            pltpu.VMEM((4, 15, 8, TILE), F32),
            pltpu.VMEM((4, RANK, 2 * RANK), F32),
            dma((sum(map(len, CHUNKS)), 3)),
            dma((NBLK,)), dma((NBLK,)), dma((NBLK,)), dma((NBLK,)), dma((NBLK,)), dma((NBLK,)), dma((NBLK,)), dma((NBLK,)), dma(()), dma(()),
            dma((4,)), dma((4,)), dma((4,)), dma((4,)), dma((4,)), dma((4, 4)), dma((4, 3)), dma((4, 3)), dma((4, 4)), dma((4, 4)),
        ],
        compiler_params=pltpu.CompilerParams(collective_id=0, has_side_effects=True, vmem_limit_bytes=52 << 20),
        name="exchange",
    )(grads[0], errors[0], q_start.T)
    new_errors, p_t, q_t = pl.pallas_call(
        finish,
        out_shape=(jax.ShapeDtypeStruct((ROWS, COLS), F32), jax.ShapeDtypeStruct((RANK, ROWS), F32), jax.ShapeDtypeStruct((RANK, COLS), F32)),
        in_specs=[vmem] * 5,
        out_specs=(hbm,) * 3,
        scratch_shapes=[pltpu.VMEM((ROWS, COLS), F32), pltpu.VMEM((RANK, COLS), F32), dma((len(PIECES), 3))],
        compiler_params=pltpu.CompilerParams(vmem_limit_bytes=24 << 20),
        name="finish",
    )(*parts)
    return new_errors[None], p_t.T, q_t.T


def solution(mesh):
    return jax.shard_map(
        local,
        mesh=mesh,
        in_specs=(P("dp", "tensor", None), P("dp", "tensor", None), P()),
        out_specs=(P("dp", "tensor", None), P("tensor", None), P()),
        check_vma=False,
    )
```

```python
import jax
import jax.numpy as jnp
from jax import lax
from jax.experimental import pallas as pl
from jax.experimental.pallas import tpu as pltpu
from jax.sharding import PartitionSpec as P

MESH = pl.DeviceIdType.MESH
F32, BF16 = jnp.float32, jnp.bfloat16
HIGH = lax.Precision.HIGHEST
ROWS, COLS, RANK, HALF = 256, 8192, 64, 32
BLK = 128
NBLK = ROWS // BLK
CHUNKS = ((1024,) * 8, (1024,) * 7 + (512, 256, 256))
OWN = COLS // 2
SLAB = OWN // 4
STRIP = SLAB // 4
TILE = 128
GROUPS = 4
GROUP = 16
PIECES = (512,) * 16
AROUND = [(a, b, c) for a in range(4) for b in range(4) for c in range(4) if (a, b, c) != (0, 0, 0) and 0 in (a, b, c)]


def split(value):
    high = value.astype(BF16)
    return high, (value - high.astype(F32)).astype(BF16)


def mod4(value):
    return jnp.where(value > 3, value - 4, value)


def device(x, y, z, c):
    return ((y * 4 + z) * 2 + c, x)


def dot_nt(a, b, precision=None):
    return lax.dot_general(a, b, (((1,), (1,)), ((), ())), precision=precision, preferred_element_type=F32)


def exchange(g_hbm, e_hbm, q_hbm, m_ref, z_ref, p_ref, pcat_ref, wcat_ref,
             ebuf, qbuf, qs, hm, mrx, hm2, spart, sprx, srx, s_ref, zbuf, rx1, ph2, rx2, gsl,
             in_sem, m_send, m_recv, p_send, p_recv, s_send, s_recv, sp_send, sp_recv, g_send, g_recv,
             r1_send, r1_recv, r2_send, r2_recv, a1_send, a1_recv, a2_send, a2_recv, f_send, f_recv):
    d = lax.axis_index("dp")
    x = lax.axis_index("tensor")
    y, z, c = lax.div(d, 8), lax.rem(lax.div(d, 2), 4), lax.rem(d, 2)
    me = y * 4 + z
    partner = device(x, y, z, 1 - c)
    mine = pl.multiple_of(c * HALF, HALF)
    other = pl.multiple_of((1 - c) * HALF, HALF)
    own = pl.multiple_of(c * OWN, OWN)
    theirs = pl.multiple_of((1 - c) * OWN, OWN)

    def remote(src, dst, send, recv, target):
        return pltpu.make_async_remote_copy(src_ref=src, dst_ref=dst, send_sem=send, recv_sem=recv, device_id=target, device_id_type=MESH)

    def all_of(ref, sem):
        pltpu.make_async_copy(ref, ref, sem).wait()

    loads = {}
    for b in range(NBLK):
        begin = 0
        for k, size in enumerate(CHUNKS[b]):
            rows, cols = pl.ds(b * BLK, BLK), pl.ds(begin, size)
            sems = in_sem.at[b * len(CHUNKS[0]) + k]
            parts = [
                pltpu.make_async_copy(g_hbm.at[rows, cols], m_ref.at[rows, cols], sems.at[0]),
                pltpu.make_async_copy(e_hbm.at[rows, cols], ebuf.at[rows, cols], sems.at[1]),
            ]
            if b == 0:
                parts.append(pltpu.make_async_copy(q_hbm.at[:, cols], qbuf.at[:, cols], sems.at[2]))
            for part in parts:
                part.start()
            loads[b, k] = begin, size, parts
            begin += size

    barrier = pltpu.get_barrier_semaphore()
    pl.semaphore_signal(barrier, inc=1, device_id=partner, device_id_type=MESH)
    for dx, dy, dz in AROUND:
        pl.semaphore_signal(barrier, inc=1, device_id=device(mod4(x + dx), mod4(y + dy), mod4(z + dz), c), device_id_type=MESH)

    def left_chunk(b, k):
        begin, size, parts = loads[b, k]
        for part in parts:
            part.wait()
        rows = slice(b * BLK, (b + 1) * BLK)
        for i in range(0, size, 256):
            cols = slice(begin + i, begin + i + 256)
            if b == 0:
                qs[0:RANK, cols], qs[RANK:, cols] = split(qbuf[:, cols])
            merged = m_ref[rows, cols] + ebuf[rows, cols]
            m_ref[rows, cols] = merged
            hm[k % 2, 0:BLK, i:i + 256], hm[k % 2, BLK:, i:i + 256] = split(merged)
        return dot_nt(qs[:, begin:begin + size], hm[k % 2, :, :size])

    def pair_copy(b):
        return remote(spart.at[b, pl.ds(other, HALF)], sprx.at[b], p_send.at[b], p_recv.at[b], partner)

    def merged_copy(b):
        rows = pl.ds(b * BLK, BLK)
        return remote(m_ref.at[rows, pl.ds(theirs, OWN)], mrx.at[rows], m_send.at[b], m_recv.at[b], partner)

    def left_send(b):
        pair_copy(b).wait()
        srx[b, me] = spart[b, pl.ds(mine, HALF)] + sprx[b]

        @pl.loop(1, 16)
        def _(r):
            target = device(x, mod4(y + lax.div(r, 4)), mod4(z + lax.rem(r, 4)), c)
            remote(srx.at[b, me], srx.at[b, me], s_send.at[b], s_recv.at[b], target).start()

    for b in range(NBLK):
        total = jnp.zeros((2 * RANK, 2 * BLK), F32)
        for k in range(len(CHUNKS[b])):
            total = total + left_chunk(b, k)
            if b > 0 and k == 1:
                left_send(b - 1)
        total = total[:RANK] + total[RANK:]
        spart[b] = total[:, :BLK] + total[:, BLK:]
        if b == 0:
            pl.semaphore_wait(barrier, 1 + len(AROUND))
        pair_copy(b).start()
        merged_copy(b).start()
    left_send(NBLK - 1)

    def left_sum(b):
        fifteen = srx.at[b, pl.ds(0, 15)]
        all_of(fifteen, s_recv.at[b])
        total = srx[b, 0]
        for r in range(1, 16):
            total = total + srx[b, r]
        place = (pl.ds(mine, HALF), pl.ds(b * BLK, BLK))
        s_ref[pl.ds(mine, HALF), b * BLK:(b + 1) * BLK] = total * (1.0 / 32)
        copy = remote(s_ref.at[place], s_ref.at[place], sp_send.at[b], sp_recv.at[b], partner)
        copy.start()
        return copy, total * (1.0 / 32)

    def chip_sum(b):
        merged_copy(b).wait()

        @pl.loop(0, OWN // 256, unroll=4)
        def _(i):
            here = pl.ds(pl.multiple_of(i * 256, 256), 256)
            there = pl.ds(pl.multiple_of(own + i * 256, 256), 256)
            rows = slice(b * BLK, (b + 1) * BLK)
            hm2[b, 0:BLK, here], hm2[b, BLK:, here] = split(m_ref[rows, there] + mrx[rows, here])

    def left_ready(b, copy):
        copy.wait()
        return s_ref[:, b * BLK:(b + 1) * BLK]

    def right_part(b, left, cols):
        both = jnp.concatenate(split(left), axis=0)
        total = jnp.dot(jnp.concatenate([both, both], axis=1), hm2[b, :, cols], preferred_element_type=F32)
        return total[:left.shape[0]] + total[left.shape[0]:]

    copy, _ = left_sum(0)
    chip_sum(0)
    left = left_ready(0, copy)
    for i in range(0, OWN, 512):
        zbuf[:, i:i + 512] = right_part(0, left, slice(i, i + 512))
    chip_sum(1)
    copy, left = left_sum(1)

    def turned(g):
        axis = jnp.where(c == 0, jnp.where(g > 2, 0, g), jnp.where(g > 2, 1, 2 - g))
        return lambda a, b, c: jnp.where(axis == 0, a, jnp.where(axis == 1, b, c))

    def placed(g):
        pick = turned(g)
        return pick(x, y, z), pick(y, z, x), pick(z, x, y)

    def moved(g, da, db, dc):
        pick = turned(g)
        dx, dy, dz = pick(da, dc, db), pick(db, da, dc), pick(dc, db, da)
        return device(mod4(x + dx), mod4(y + dy), mod4(z + dz), c)

    def group_rows(g, row=0, rows=GROUP):
        return pl.ds(pl.multiple_of(mod4(2 * c + g) * GROUP + row, rows), rows)

    for half in range(2):
        if half:
            copy.wait()
            left = s_ref[pl.ds(other, HALF), BLK:]
        ranks = pl.ds(other if half else mine, HALF)
        for i in range(0, OWN, 512):
            zbuf[ranks, i:i + 512] += right_part(1, left, slice(i, i + 512))

        @pl.loop(0, 6)
        def _(i):
            step = jnp.where(i < 2, 2, jnp.where(i < 4, 1, 3))
            g = 2 * half + lax.rem(i, 2)
            k = mod4(placed(g)[0] + step)
            src = zbuf.at[group_rows(g), pl.ds(pl.multiple_of(k * SLAB, SLAB), SLAB)]
            remote(src, rx1.at[g, step - 1], r1_send.at[g], r1_recv.at[g], moved(g, step, 0, 0)).start()

    sketch = s_ref[...]
    gsl[x] = jnp.concatenate([dot_nt(sketch, sketch, HIGH), jnp.zeros((RANK, RANK), F32)], axis=1)
    for k in range(3):
        remote(gsl.at[x], gsl.at[x], g_send, g_recv, device(mod4(x + k + 1), y, z, c)).start()

    def tile_of(v, w):
        return pl.ds(pl.multiple_of(lax.rem(w, 2) * 8, 8), 8), pl.multiple_of((v * 2 + lax.div(w, 2)) * TILE, TILE)

    @pl.loop(0, GROUPS)
    def _(g):
        first, second, third = placed(g)
        all_of(rx1.at[g], r1_recv.at[g])
        cols = pl.ds(pl.multiple_of(first * SLAB, SLAB), SLAB)
        ph2[g] = (zbuf[group_rows(g), cols] + rx1[g, 0]) + (rx1[g, 1] + rx1[g, 2])

        @pl.loop(1, 16)
        def _(r):
            db, dc = lax.div(r, 4), lax.rem(r, 4)
            rows, col = tile_of(mod4(second + db), mod4(third + dc))
            remote(ph2.at[g, rows, pl.ds(col, TILE)], rx2.at[g, r - 1], r2_send.at[g], r2_recv.at[g], moved(g, 0, db, dc)).start()

    three = gsl.at[pl.ds(0, 3)]
    all_of(three, g_recv)
    gram = (gsl[0] + gsl[1]) + (gsl[2] + gsl[3])
    lane = lax.broadcasted_iota(jnp.int32, (RANK, 2 * RANK), 1)
    sub = lax.broadcasted_iota(jnp.int32, (RANK, 2 * RANK), 0)
    diagonal = jnp.where(lane == sub, gram, 0.0)
    trace = jnp.sum(jnp.sum(diagonal, axis=1, keepdims=True), axis=0, keepdims=True)
    mat = gram + jnp.where(lane == sub, 1e-05 * (trace / RANK), 0.0) + jnp.where(lane == sub + RANK, 1.0, 0.0)
    row_id = lax.broadcasted_iota(jnp.int32, (RANK, 1), 0)

    def eliminate(mat, begin, end):
        for j in range(begin, end):
            pivot = mat[j:j + 1, :]
            factor = jnp.where(row_id > j, mat[:, j:j + 1] / mat[j:j + 1, j:j + 1], 0.0)
            mat = mat - factor * pivot
        return mat

    mat = eliminate(mat, 0, RANK // 2)

    @pl.loop(0, GROUPS)
    def _(g):
        first, second, third = placed(g)
        all_of(rx2.at[g], r2_recv.at[g])
        rows, col = tile_of(second, third)
        total = ph2[g, rows, pl.ds(col, TILE)]
        for r in range(15):
            total = total + rx2[g, r]
        rows = group_rows(g, lax.rem(third, 2) * 8, 8)
        place = (rows, pl.ds(pl.multiple_of(own + first * SLAB + col, TILE), TILE))
        z_ref[place] = total

        @pl.loop(1, 16)
        def _(r):
            db, dc = lax.div(r, 4), lax.rem(r, 4)
            remote(z_ref.at[place], z_ref.at[place], a1_send.at[g], a1_recv.at[g, db], moved(g, 0, db, dc)).start()

    mat = eliminate(mat, RANK // 2, RANK)
    scale = jnp.sum(jnp.where(lane == sub, mat, 0.0), axis=1, keepdims=True)
    inverse = mat[:, RANK:] / jnp.sqrt(scale)
    parts = jnp.concatenate(split(inverse * (1.0 / 32)), axis=0)
    wcat_ref[...] = jnp.concatenate([parts, parts], axis=1)

    def slab(g, v):
        return z_ref.at[group_rows(g), pl.ds(pl.multiple_of(own + v * SLAB, SLAB), SLAB)]

    def forward(g, step):
        here = slab(g, mod4(placed(g)[0] + step))
        return remote(here, here, f_send.at[g, step], f_recv.at[g, step], partner)

    def along(g, step, away):
        first, second, _ = placed(g)
        cols = pl.ds(pl.multiple_of(own + first * SLAB + mod4(second + 4 - away) * STRIP, STRIP), STRIP)
        here = z_ref.at[group_rows(g), cols]
        return remote(here, here, a2_send.at[g, step - 1], a2_recv.at[g, step - 1], moved(g, step, 0, 0))

    def strip_on(g, away, tiles):
        all_of(z_ref.at[pl.ds(0, 8), pl.ds(0, tiles * TILE)], a1_recv.at[g, away])
        for step in (2, 1, 3):
            along(g, step, away).start()

    @pl.loop(0, GROUPS)
    def _(g):
        strip_on(g, 0, 3)

    @pl.loop(0, 3 * GROUPS)
    def _(i):
        strip_on(lax.rem(i, 4), jnp.where(i < 4, 1, jnp.where(i < 8, 3, 2)), 4)

    @pl.loop(0, GROUPS)
    def _(g):
        forward(g, 0).start()

    p_t = jnp.dot(inverse, sketch, precision=HIGH, preferred_element_type=F32)
    p_ref[...] = p_t
    high, mid = split(p_t.T)
    pcat_ref[...] = jnp.concatenate([high, high, mid], axis=1)
    @pl.loop(0, 3 * GROUPS)
    def _(i):
        g, step = lax.rem(i, 4), jnp.where(i < 4, 1, jnp.where(i < 8, 3, 2))
        all_of(slab(g, 0), a2_recv.at[g, step - 1])
        forward(g, 4 - step).start()

    for b in range(NBLK):
        all_of(srx.at[b, pl.ds(0, 15)], s_send.at[b])
    all_of(three, g_send)

    @pl.loop(0, GROUPS)
    def _(g):
        all_of(rx1.at[g], r1_send.at[g])
        all_of(rx2.at[g], r2_send.at[g])
        all_of(z_ref.at[pl.ds(0, 8), pl.ds(0, 15 * TILE)], a1_send.at[g])
        for step in range(3):
            all_of(slab(g, 0), a2_send.at[g, step])

    @pl.loop(0, 4 * GROUPS)
    def _(i):
        forward(lax.rem(i, 4), lax.div(i, 4)).wait()


def finish(m_ref, z_ref, p_ref, pcat_ref, wcat_ref, n_hbm, p_hbm, q_hbm, nbuf, qbuf, sem):
    copies = []

    def write(k, cols, q3):
        nbuf[:, cols] = m_ref[:, cols] - jnp.dot(pcat_ref[...], q3, preferred_element_type=F32)
        copies.append(pltpu.make_async_copy(nbuf.at[:, cols], n_hbm.at[:, cols], sem.at[k, 0]))
        copies[-1].start()

    begin, last = 0, None
    for k, size in enumerate(PIECES):
        cols = pl.ds(begin, size)
        begin += size
        q = jnp.dot(wcat_ref[...], jnp.concatenate(split(z_ref[:, cols]), axis=0), preferred_element_type=F32)
        q = q[:RANK] + q[RANK:]
        qbuf[:, cols] = q
        high, mid = split(q)
        q3 = jnp.concatenate([high, mid, high], axis=0)
        if last is not None:
            write(*last)
        last = (k, cols, q3)
    copies.append(pltpu.make_async_copy(qbuf, q_hbm, sem.at[0, 1]))
    copies[-1].start()
    write(*last)
    copies.append(pltpu.make_async_copy(p_ref, p_hbm, sem.at[0, 2]))
    copies[-1].start()
    for copy in copies:
        copy.wait()


def local(grads, errors, q_start):
    vmem = pl.BlockSpec(memory_space=pltpu.VMEM)
    hbm = pl.BlockSpec(memory_space=pl.ANY)
    dma = pltpu.SemaphoreType.DMA
    parts = pl.pallas_call(
        exchange,
        out_shape=(
            pltpu.VMEM((ROWS, COLS), F32), pltpu.VMEM((RANK, COLS), F32), pltpu.VMEM((RANK, ROWS), F32),
            pltpu.VMEM((ROWS, 3 * RANK), BF16), pltpu.VMEM((2 * RANK, 2 * RANK), BF16),
        ),
        in_specs=[hbm] * 3,
        out_specs=(vmem,) * 5,
        scratch_shapes=[
            pltpu.VMEM((ROWS, COLS), F32),
            pltpu.VMEM((RANK, COLS), F32),
            pltpu.VMEM((2 * RANK, COLS), BF16),
            pltpu.VMEM((2, 2 * BLK, max(CHUNKS[0])), BF16),
            pltpu.VMEM((ROWS, OWN), F32),
            pltpu.VMEM((NBLK, 2 * BLK, OWN), BF16),
            pltpu.VMEM((NBLK, RANK, BLK), F32),
            pltpu.VMEM((NBLK, HALF, BLK), F32),
            pltpu.VMEM((NBLK, 16, HALF, BLK), F32),
            pltpu.VMEM((RANK, ROWS), F32),
            pltpu.VMEM((RANK, OWN), F32),
            pltpu.VMEM((4, 3, GROUP, SLAB), F32),
            pltpu.VMEM((4, GROUP, SLAB), F32),
            pltpu.VMEM((4, 15, 8, TILE), F32),
            pltpu.VMEM((4, RANK, 2 * RANK), F32),
            dma((sum(map(len, CHUNKS)), 3)),
            dma((NBLK,)), dma((NBLK,)), dma((NBLK,)), dma((NBLK,)), dma((NBLK,)), dma((NBLK,)), dma((NBLK,)), dma((NBLK,)), dma(()), dma(()),
            dma((4,)), dma((4,)), dma((4,)), dma((4,)), dma((4,)), dma((4, 4)), dma((4, 3)), dma((4, 3)), dma((4, 4)), dma((4, 4)),
        ],
        compiler_params=pltpu.CompilerParams(collective_id=0, has_side_effects=True, vmem_limit_bytes=52 << 20),
        name="exchange",
    )(grads[0], errors[0], q_start.T)
    new_errors, p_t, q_t = pl.pallas_call(
        finish,
        out_shape=(jax.ShapeDtypeStruct((ROWS, COLS), F32), jax.ShapeDtypeStruct((RANK, ROWS), F32), jax.ShapeDtypeStruct((RANK, COLS), F32)),
        in_specs=[vmem] * 5,
        out_specs=(hbm,) * 3,
        scratch_shapes=[pltpu.VMEM((ROWS, COLS), F32), pltpu.VMEM((RANK, COLS), F32), dma((len(PIECES), 3))],
        compiler_params=pltpu.CompilerParams(vmem_limit_bytes=24 << 20),
        name="finish",
    )(*parts)
    return new_errors[None], p_t.T, q_t.T


def solution(mesh):
    return jax.shard_map(
        local,
        mesh=mesh,
        in_specs=(P("dp", "tensor", None), P("dp", "tensor", None), P()),
        out_specs=(P("dp", "tensor", None), P("tensor", None), P()),
        check_vma=False,
    )
```

```python
import jax
import jax.numpy as jnp
from jax import lax
from jax.experimental import pallas as pl
from jax.experimental.pallas import tpu as pltpu
from jax.sharding import PartitionSpec as P

MESH = pl.DeviceIdType.MESH
F32, BF16 = jnp.float32, jnp.bfloat16
HIGH = lax.Precision.HIGHEST
ROWS, COLS, RANK, HALF = 256, 8192, 64, 32
BLK = 128
NBLK = ROWS // BLK
CHUNKS = ((1024,) * 8, (1024,) * 7 + (512, 256, 256))
OWN = COLS // 2
SLAB = OWN // 4
STRIP = SLAB // 4
TILE = 128
GROUPS = 4
GROUP = 16
PIECES = (512,) * 16
AROUND = [(a, b, c) for a in range(4) for b in range(4) for c in range(4) if (a, b, c) != (0, 0, 0) and 0 in (a, b, c)]


def split(value):
    high = value.astype(BF16)
    return high, (value - high.astype(F32)).astype(BF16)


def mod4(value):
    return jnp.where(value > 3, value - 4, value)


def device(x, y, z, c):
    return ((y * 4 + z) * 2 + c, x)


def dot_nt(a, b, precision=None):
    return lax.dot_general(a, b, (((1,), (1,)), ((), ())), precision=precision, preferred_element_type=F32)


def exchange(g_hbm, e_hbm, q_hbm, m_ref, z_ref, p_ref, pcat_ref, wcat_ref,
             ebuf, qbuf, qs, hm, mrx, hm2, spart, sprx, srx, s_ref, zbuf, rx1, ph2, rx2, gsl,
             in_sem, m_send, m_recv, p_send, p_recv, s_send, s_recv, sp_send, sp_recv, g_send, g_recv,
             r1_send, r1_recv, r2_send, r2_recv, a1_send, a1_recv, a2_send, a2_recv, f_send, f_recv):
    d = lax.axis_index("dp")
    x = lax.axis_index("tensor")
    y, z, c = lax.div(d, 8), lax.rem(lax.div(d, 2), 4), lax.rem(d, 2)
    me = y * 4 + z
    partner = device(x, y, z, 1 - c)
    mine = pl.multiple_of(c * HALF, HALF)
    other = pl.multiple_of((1 - c) * HALF, HALF)
    own = pl.multiple_of(c * OWN, OWN)
    theirs = pl.multiple_of((1 - c) * OWN, OWN)

    def remote(src, dst, send, recv, target):
        return pltpu.make_async_remote_copy(src_ref=src, dst_ref=dst, send_sem=send, recv_sem=recv, device_id=target, device_id_type=MESH)

    def all_of(ref, sem):
        pltpu.make_async_copy(ref, ref, sem).wait()

    loads = {}
    for b in range(NBLK):
        begin = 0
        for k, size in enumerate(CHUNKS[b]):
            rows, cols = pl.ds(b * BLK, BLK), pl.ds(begin, size)
            sems = in_sem.at[b * len(CHUNKS[0]) + k]
            parts = [
                pltpu.make_async_copy(g_hbm.at[rows, cols], m_ref.at[rows, cols], sems.at[0]),
                pltpu.make_async_copy(e_hbm.at[rows, cols], ebuf.at[rows, cols], sems.at[1]),
            ]
            if b == 0:
                parts.append(pltpu.make_async_copy(q_hbm.at[:, cols], qbuf.at[:, cols], sems.at[2]))
            for part in parts:
                part.start()
            loads[b, k] = begin, size, parts
            begin += size

    barrier = pltpu.get_barrier_semaphore()
    pl.semaphore_signal(barrier, inc=1, device_id=partner, device_id_type=MESH)
    for dx, dy, dz in AROUND:
        pl.semaphore_signal(barrier, inc=1, device_id=device(mod4(x + dx), mod4(y + dy), mod4(z + dz), c), device_id_type=MESH)

    def left_chunk(b, k):
        begin, size, parts = loads[b, k]
        for part in parts:
            part.wait()
        rows = slice(b * BLK, (b + 1) * BLK)
        for i in range(0, size, 256):
            cols = slice(begin + i, begin + i + 256)
            if b == 0:
                qs[0:RANK, cols], qs[RANK:, cols] = split(qbuf[:, cols])
            merged = m_ref[rows, cols] + ebuf[rows, cols]
            m_ref[rows, cols] = merged
            hm[k % 2, 0:BLK, i:i + 256], hm[k % 2, BLK:, i:i + 256] = split(merged)
        return dot_nt(qs[:, begin:begin + size], hm[k % 2, :, :size])

    def pair_copy(b):
        return remote(spart.at[b, pl.ds(other, HALF)], sprx.at[b], p_send.at[b], p_recv.at[b], partner)

    def merged_copy(b):
        rows = pl.ds(b * BLK, BLK)
        return remote(m_ref.at[rows, pl.ds(theirs, OWN)], mrx.at[rows], m_send.at[b], m_recv.at[b], partner)

    def left_send(b):
        pair_copy(b).wait()
        srx[b, me] = spart[b, pl.ds(mine, HALF)] + sprx[b]

        @pl.loop(1, 16)
        def _(r):
            target = device(x, mod4(y + lax.div(r, 4)), mod4(z + lax.rem(r, 4)), c)
            remote(srx.at[b, me], srx.at[b, me], s_send.at[b], s_recv.at[b], target).start()

    for b in range(NBLK):
        total = jnp.zeros((2 * RANK, 2 * BLK), F32)
        for k in range(len(CHUNKS[b])):
            total = total + left_chunk(b, k)
            if b > 0 and k == 1:
                left_send(b - 1)
        total = total[:RANK] + total[RANK:]
        spart[b] = total[:, :BLK] + total[:, BLK:]
        if b == 0:
            pl.semaphore_wait(barrier, 1 + len(AROUND))
        pair_copy(b).start()
        merged_copy(b).start()
    left_send(NBLK - 1)

    def left_sum(b):
        fifteen = srx.at[b, pl.ds(0, 15)]
        all_of(fifteen, s_recv.at[b])
        total = srx[b, 0]
        for r in range(1, 16):
            total = total + srx[b, r]
        place = (pl.ds(mine, HALF), pl.ds(b * BLK, BLK))
        s_ref[pl.ds(mine, HALF), b * BLK:(b + 1) * BLK] = total * (1.0 / 32)
        copy = remote(s_ref.at[place], s_ref.at[place], sp_send.at[b], sp_recv.at[b], partner)
        copy.start()
        return copy, total * (1.0 / 32)

    def chip_sum(b):
        merged_copy(b).wait()

        @pl.loop(0, OWN // 256, unroll=4)
        def _(i):
            here = pl.ds(pl.multiple_of(i * 256, 256), 256)
            there = pl.ds(pl.multiple_of(own + i * 256, 256), 256)
            rows = slice(b * BLK, (b + 1) * BLK)
            hm2[b, 0:BLK, here], hm2[b, BLK:, here] = split(m_ref[rows, there] + mrx[rows, here])

    def left_ready(b, copy):
        copy.wait()
        return s_ref[:, b * BLK:(b + 1) * BLK]

    def right_part(b, left, cols):
        both = jnp.concatenate(split(left), axis=0)
        total = jnp.dot(jnp.concatenate([both, both], axis=1), hm2[b, :, cols], preferred_element_type=F32)
        return total[:left.shape[0]] + total[left.shape[0]:]

    copy, _ = left_sum(0)
    chip_sum(0)
    left = left_ready(0, copy)
    for i in range(0, OWN, 512):
        zbuf[:, i:i + 512] = right_part(0, left, slice(i, i + 512))
    chip_sum(1)
    copy, left = left_sum(1)

    def turned(g):
        axis = jnp.where(c == 0, jnp.where(g > 2, 0, g), jnp.where(g > 2, 1, 2 - g))
        return lambda a, b, c: jnp.where(axis == 0, a, jnp.where(axis == 1, b, c))

    def placed(g):
        pick = turned(g)
        return pick(x, y, z), pick(y, z, x), pick(z, x, y)

    def moved(g, da, db, dc):
        pick = turned(g)
        dx, dy, dz = pick(da, dc, db), pick(db, da, dc), pick(dc, db, da)
        return device(mod4(x + dx), mod4(y + dy), mod4(z + dz), c)

    def group_rows(g, row=0, rows=GROUP):
        return pl.ds(pl.multiple_of(mod4(2 * c + g) * GROUP + row, rows), rows)

    for half in range(2):
        if half:
            copy.wait()
            left = s_ref[pl.ds(other, HALF), BLK:]
        ranks = pl.ds(other if half else mine, HALF)
        for i in range(0, OWN, 512):
            zbuf[ranks, i:i + 512] += right_part(1, left, slice(i, i + 512))

        @pl.loop(0, 6)
        def _(i):
            turn = lax.rem(i, 3)
            step = jnp.where(turn == 0, 2, jnp.where(turn == 1, 1, 3))
            g = 2 * half + lax.div(i, 3)
            k = mod4(placed(g)[0] + step)
            src = zbuf.at[group_rows(g), pl.ds(pl.multiple_of(k * SLAB, SLAB), SLAB)]
            remote(src, rx1.at[g, step - 1], r1_send.at[g], r1_recv.at[g], moved(g, step, 0, 0)).start()

    sketch = s_ref[...]
    gsl[x] = jnp.concatenate([dot_nt(sketch, sketch, HIGH), jnp.zeros((RANK, RANK), F32)], axis=1)
    for k in range(3):
        remote(gsl.at[x], gsl.at[x], g_send, g_recv, device(mod4(x + k + 1), y, z, c)).start()

    def tile_of(v, w):
        return pl.ds(pl.multiple_of(lax.rem(w, 2) * 8, 8), 8), pl.multiple_of((v * 2 + lax.div(w, 2)) * TILE, TILE)

    @pl.loop(0, GROUPS)
    def _(g):
        first, second, third = placed(g)
        all_of(rx1.at[g], r1_recv.at[g])
        cols = pl.ds(pl.multiple_of(first * SLAB, SLAB), SLAB)
        ph2[g] = (zbuf[group_rows(g), cols] + rx1[g, 0]) + (rx1[g, 1] + rx1[g, 2])

        @pl.loop(1, 16)
        def _(r):
            db, dc = lax.div(r, 4), lax.rem(r, 4)
            rows, col = tile_of(mod4(second + db), mod4(third + dc))
            remote(ph2.at[g, rows, pl.ds(col, TILE)], rx2.at[g, r - 1], r2_send.at[g], r2_recv.at[g], moved(g, 0, db, dc)).start()

    three = gsl.at[pl.ds(0, 3)]
    all_of(three, g_recv)
    gram = (gsl[0] + gsl[1]) + (gsl[2] + gsl[3])
    lane = lax.broadcasted_iota(jnp.int32, (RANK, 2 * RANK), 1)
    sub = lax.broadcasted_iota(jnp.int32, (RANK, 2 * RANK), 0)
    diagonal = jnp.where(lane == sub, gram, 0.0)
    trace = jnp.sum(jnp.sum(diagonal, axis=1, keepdims=True), axis=0, keepdims=True)
    mat = gram + jnp.where(lane == sub, 1e-05 * (trace / RANK), 0.0) + jnp.where(lane == sub + RANK, 1.0, 0.0)
    row_id = lax.broadcasted_iota(jnp.int32, (RANK, 1), 0)

    def eliminate(mat, begin, end):
        for j in range(begin, end):
            pivot = mat[j:j + 1, :]
            factor = jnp.where(row_id > j, mat[:, j:j + 1] / mat[j:j + 1, j:j + 1], 0.0)
            mat = mat - factor * pivot
        return mat

    mat = eliminate(mat, 0, RANK // 2)

    @pl.loop(0, GROUPS)
    def _(g):
        first, second, third = placed(g)
        all_of(rx2.at[g], r2_recv.at[g])
        rows, col = tile_of(second, third)
        total = ph2[g, rows, pl.ds(col, TILE)]
        for r in range(15):
            total = total + rx2[g, r]
        rows = group_rows(g, lax.rem(third, 2) * 8, 8)
        place = (rows, pl.ds(pl.multiple_of(own + first * SLAB + col, TILE), TILE))
        z_ref[place] = total

        @pl.loop(1, 16)
        def _(r):
            db, dc = lax.div(r, 4), lax.rem(r, 4)
            remote(z_ref.at[place], z_ref.at[place], a1_send.at[g], a1_recv.at[g, db], moved(g, 0, db, dc)).start()

    mat = eliminate(mat, RANK // 2, RANK)
    scale = jnp.sum(jnp.where(lane == sub, mat, 0.0), axis=1, keepdims=True)
    inverse = mat[:, RANK:] / jnp.sqrt(scale)
    parts = jnp.concatenate(split(inverse * (1.0 / 32)), axis=0)
    wcat_ref[...] = jnp.concatenate([parts, parts], axis=1)

    def slab(g, v):
        return z_ref.at[group_rows(g), pl.ds(pl.multiple_of(own + v * SLAB, SLAB), SLAB)]

    def forward(g, step):
        here = slab(g, mod4(placed(g)[0] + step))
        return remote(here, here, f_send.at[g, step], f_recv.at[g, step], partner)

    def along(g, step, away):
        first, second, _ = placed(g)
        cols = pl.ds(pl.multiple_of(own + first * SLAB + mod4(second + 4 - away) * STRIP, STRIP), STRIP)
        here = z_ref.at[group_rows(g), cols]
        return remote(here, here, a2_send.at[g, step - 1], a2_recv.at[g, step - 1], moved(g, step, 0, 0))

    def strip_on(g, away, tiles):
        all_of(z_ref.at[pl.ds(0, 8), pl.ds(0, tiles * TILE)], a1_recv.at[g, away])
        for step in (2, 1, 3):
            along(g, step, away).start()

    @pl.loop(0, GROUPS)
    def _(g):
        strip_on(g, 0, 3)

    @pl.loop(0, 3 * GROUPS)
    def _(i):
        strip_on(lax.rem(i, 4), jnp.where(i < 4, 1, jnp.where(i < 8, 3, 2)), 4)

    @pl.loop(0, GROUPS)
    def _(g):
        forward(g, 0).start()

    p_t = jnp.dot(inverse, sketch, precision=HIGH, preferred_element_type=F32)
    p_ref[...] = p_t
    high, mid = split(p_t.T)
    pcat_ref[...] = jnp.concatenate([high, high, mid], axis=1)
    @pl.loop(0, 3 * GROUPS)
    def _(i):
        g, step = lax.rem(i, 4), jnp.where(i < 4, 1, jnp.where(i < 8, 3, 2))
        all_of(slab(g, 0), a2_recv.at[g, step - 1])
        forward(g, 4 - step).start()

    for b in range(NBLK):
        all_of(srx.at[b, pl.ds(0, 15)], s_send.at[b])
    all_of(three, g_send)

    @pl.loop(0, GROUPS)
    def _(g):
        all_of(rx1.at[g], r1_send.at[g])
        all_of(rx2.at[g], r2_send.at[g])
        all_of(z_ref.at[pl.ds(0, 8), pl.ds(0, 15 * TILE)], a1_send.at[g])
        for step in range(3):
            all_of(slab(g, 0), a2_send.at[g, step])

    @pl.loop(0, 4 * GROUPS)
    def _(i):
        forward(lax.rem(i, 4), lax.div(i, 4)).wait()


def finish(m_ref, z_ref, p_ref, pcat_ref, wcat_ref, n_hbm, p_hbm, q_hbm, nbuf, qbuf, sem):
    copies = []

    def write(k, cols, q3):
        nbuf[:, cols] = m_ref[:, cols] - jnp.dot(pcat_ref[...], q3, preferred_element_type=F32)
        copies.append(pltpu.make_async_copy(nbuf.at[:, cols], n_hbm.at[:, cols], sem.at[k, 0]))
        copies[-1].start()

    begin, last = 0, None
    for k, size in enumerate(PIECES):
        cols = pl.ds(begin, size)
        begin += size
        q = jnp.dot(wcat_ref[...], jnp.concatenate(split(z_ref[:, cols]), axis=0), preferred_element_type=F32)
        q = q[:RANK] + q[RANK:]
        qbuf[:, cols] = q
        high, mid = split(q)
        q3 = jnp.concatenate([high, mid, high], axis=0)
        if last is not None:
            write(*last)
        last = (k, cols, q3)
    copies.append(pltpu.make_async_copy(qbuf, q_hbm, sem.at[0, 1]))
    copies[-1].start()
    write(*last)
    copies.append(pltpu.make_async_copy(p_ref, p_hbm, sem.at[0, 2]))
    copies[-1].start()
    for copy in copies:
        copy.wait()


def local(grads, errors, q_start):
    vmem = pl.BlockSpec(memory_space=pltpu.VMEM)
    hbm = pl.BlockSpec(memory_space=pl.ANY)
    dma = pltpu.SemaphoreType.DMA
    parts = pl.pallas_call(
        exchange,
        out_shape=(
            pltpu.VMEM((ROWS, COLS), F32), pltpu.VMEM((RANK, COLS), F32), pltpu.VMEM((RANK, ROWS), F32),
            pltpu.VMEM((ROWS, 3 * RANK), BF16), pltpu.VMEM((2 * RANK, 2 * RANK), BF16),
        ),
        in_specs=[hbm] * 3,
        out_specs=(vmem,) * 5,
        scratch_shapes=[
            pltpu.VMEM((ROWS, COLS), F32),
            pltpu.VMEM((RANK, COLS), F32),
            pltpu.VMEM((2 * RANK, COLS), BF16),
            pltpu.VMEM((2, 2 * BLK, max(CHUNKS[0])), BF16),
            pltpu.VMEM((ROWS, OWN), F32),
            pltpu.VMEM((NBLK, 2 * BLK, OWN), BF16),
            pltpu.VMEM((NBLK, RANK, BLK), F32),
            pltpu.VMEM((NBLK, HALF, BLK), F32),
            pltpu.VMEM((NBLK, 16, HALF, BLK), F32),
            pltpu.VMEM((RANK, ROWS), F32),
            pltpu.VMEM((RANK, OWN), F32),
            pltpu.VMEM((4, 3, GROUP, SLAB), F32),
            pltpu.VMEM((4, GROUP, SLAB), F32),
            pltpu.VMEM((4, 15, 8, TILE), F32),
            pltpu.VMEM((4, RANK, 2 * RANK), F32),
            dma((sum(map(len, CHUNKS)), 3)),
            dma((NBLK,)), dma((NBLK,)), dma((NBLK,)), dma((NBLK,)), dma((NBLK,)), dma((NBLK,)), dma((NBLK,)), dma((NBLK,)), dma(()), dma(()),
            dma((4,)), dma((4,)), dma((4,)), dma((4,)), dma((4,)), dma((4, 4)), dma((4, 3)), dma((4, 3)), dma((4, 4)), dma((4, 4)),
        ],
        compiler_params=pltpu.CompilerParams(collective_id=0, has_side_effects=True, vmem_limit_bytes=52 << 20),
        name="exchange",
    )(grads[0], errors[0], q_start.T)
    new_errors, p_t, q_t = pl.pallas_call(
        finish,
        out_shape=(jax.ShapeDtypeStruct((ROWS, COLS), F32), jax.ShapeDtypeStruct((RANK, ROWS), F32), jax.ShapeDtypeStruct((RANK, COLS), F32)),
        in_specs=[vmem] * 5,
        out_specs=(hbm,) * 3,
        scratch_shapes=[pltpu.VMEM((ROWS, COLS), F32), pltpu.VMEM((RANK, COLS), F32), dma((len(PIECES), 3))],
        compiler_params=pltpu.CompilerParams(vmem_limit_bytes=24 << 20),
        name="finish",
    )(*parts)
    return new_errors[None], p_t.T, q_t.T


def solution(mesh):
    return jax.shard_map(
        local,
        mesh=mesh,
        in_specs=(P("dp", "tensor", None), P("dp", "tensor", None), P()),
        out_specs=(P("dp", "tensor", None), P("tensor", None), P()),
        check_vma=False,
    )
```
